512 devices in a mesh: grp: 16 (over y_hi, x, core), seq: 32 (over z, y_lo).
Axes of the slice: x: 4, y: 4 (y_hi: 2, y_lo: 2; y = y_hi * 2 + y_lo), z: 16, core: 2. Of those that a mesh axis runs over, the one named last changes fastest.
Arguments:
- prompt_states: bfloat16 [3072, 5120], P('seq'), may hold values from -6 to 6
- step_states: bfloat16 [4, 16, 5120], replicated, may hold values from -6 to 6
- norm_gain: float32 [5120], replicated, may hold values from 0.1 to 1.9
- w_query: bfloat16 [5120, 8192], P('seq', 'grp'), may hold values from -0.078125 to 0.078125
- key_weight: bfloat16 [5120, 1024], P('seq'), may hold values from -0.078125 to 0.078125
- value_weight: bfloat16 [5120, 1024], P('seq'), may hold values from -0.078125 to 0.078125
- q_gain: float32 [128], replicated, may hold values from 0.5 to 14, as said below
- k_gain: float32 [128], replicated, may hold values from 0.5 to 14, as said below
Outputs:
- prompt_context: bfloat16 [3072, 8192], P('seq', 'grp')
- step_context: bfloat16 [4, 16, 8192], P(None, 'grp', 'seq')
The draws below stay inside these ranges and needn't reach their ends.
Inputs may be any that keep to these rules, and one draw needn't show every extreme that they name: `q_gain`: positive gain of each query dimension. `k_gain`: positive gain of each key dimension.
All inputs are finite; a program needn't handle non-finite values.
Results may differ from the reference program's by a relative error of at most 0.013.
The reference program's roundings to bfloat16 on the way count: a program that leaves them out, or rounds other values in their place, can miss the bound.
Values may be sent and summed in bfloat16 or wider, within the bound.
No kernel may reach another device: no remote copies, remote signals or barrier semaphores. Data moves between devices by JAX's collectives and lax.ppermute only.
A program may use at most 64 MiB of HBM per device.

```python
import math
import jax
import jax.numpy as jnp
from jax import lax

MODEL_DIM = 5120
QUERY_HEADS = 64
KEY_VALUE_HEADS = 8
HEAD_DIM = 128
STEPS = 4
PROMPT_TOKENS = 3072
RESP = 16


def spread_gain(key, lower, upper):
    return jnp.exp(jax.random.uniform(key, (HEAD_DIM,), jnp.float32, jnp.log(lower), jnp.log(upper)))


def draw_q_gain(key, part):
    own_key = jax.random.fold_in(key, 5)
    return spread_gain(own_key, 0.5, 2.0)


def draw_k_gain(key, part):
    own_key = jax.random.fold_in(key, 9)
    return spread_gain(own_key, 0.5, 2.0)


def level_of(key, dims, shards, low, high):
    level = 1.0
    for dim, parts in shards:
        steps = jax.random.uniform(jax.random.fold_in(jax.random.fold_in(key, 6), dim), (parts,), jnp.float32, low / len(shards), high / len(shards))
        level = level * jnp.repeat(jnp.exp(steps), dims[dim] // parts).reshape((-1,) + (1,) * (len(dims) - 1 - dim))
    return level


def bell_draw(stream_key, shape, deviation, limit, pieces=(), kind=jnp.bfloat16):
    values = deviation * jax.random.normal(stream_key, shape, jnp.float32)
    if pieces:
        values = values * level_of(stream_key, shape, pieces, -0.22, 0.18)
    return jnp.clip(values, -limit, limit).astype(kind)


def setup_inputs(seed: int = 0) -> dict:
    arg_keys = jax.random.split(jax.random.key(seed), 9)
    return {
        "prompt_states": bell_draw(arg_keys[0], (PROMPT_TOKENS, MODEL_DIM), 1.0, 6.0, ((0, 32),)),
        "step_states": bell_draw(arg_keys[1], (STEPS, RESP, MODEL_DIM), 1.0, 6.0),
        "norm_gain": jnp.clip(1.0 + 0.18 * jax.random.normal(arg_keys[2], (MODEL_DIM,), jnp.float32), 0.1, 1.9),
        "w_query": bell_draw(arg_keys[3], (MODEL_DIM, QUERY_HEADS * HEAD_DIM), MODEL_DIM ** -0.5, 0.078125, ((0, 32), (1, 16))),
        "key_weight": bell_draw(arg_keys[4], (MODEL_DIM, KEY_VALUE_HEADS * HEAD_DIM), MODEL_DIM ** -0.5, 0.078125, ((0, 32),)),
        "value_weight": bell_draw(arg_keys[5], (MODEL_DIM, KEY_VALUE_HEADS * HEAD_DIM), MODEL_DIM ** -0.5, 0.078125, ((0, 32),)),
        "q_gain": draw_q_gain(jax.random.fold_in(arg_keys[8], 71), 0),
        "k_gain": draw_k_gain(jax.random.fold_in(arg_keys[8], 71), 0),
    }


EPS = 1e-06
THETA = 1000000.0

def rms_scale(values_in, gain):
    return values_in * lax.rsqrt(lax.optimization_barrier(jnp.mean(values_in * values_in, axis=-1, keepdims=True)) + EPS) * gain

def apply_rotary(values_in, positions):
    half_size = values_in.shape[-1] // 2
    freqs = jnp.power(jnp.float32(THETA), -jnp.arange(half_size, dtype=jnp.float32) / half_size)
    angles = positions.astype(jnp.float32)[:, None] * freqs[None, :]
    cosine = jnp.cos(angles)[:, None, :]
    sine = jnp.sin(angles)[:, None, :]
    first_half = values_in[..., :half_size]
    second_half = values_in[..., half_size:]
    return jnp.concatenate([first_half * cosine - second_half * sine, second_half * cosine + first_half * sine], axis=-1)

def reference(prompt_states, step_states, norm_gain, w_query, key_weight, value_weight, q_gain, k_gain):
    query_group_width = QUERY_HEADS // KEY_VALUE_HEADS
    scaling = 1.0 / math.sqrt(HEAD_DIM)
    decode_rows = STEPS * RESP
    all_rows = jnp.concatenate([prompt_states, step_states.reshape(decode_rows, MODEL_DIM)], axis=0)
    overall_rows = all_rows.shape[0]
    positions = jnp.concatenate([jnp.arange(PROMPT_TOKENS, dtype=jnp.int32), PROMPT_TOKENS + jnp.arange(decode_rows, dtype=jnp.int32) // RESP])
    normalized_input = rms_scale(all_rows.astype(jnp.float32), norm_gain).astype(jnp.bfloat16)
    raw_query = jnp.dot(normalized_input, w_query, preferred_element_type=jnp.float32).reshape(overall_rows, QUERY_HEADS, HEAD_DIM)
    unrotated_key = jnp.dot(normalized_input, key_weight, preferred_element_type=jnp.float32).reshape(overall_rows, KEY_VALUE_HEADS, HEAD_DIM)
    projected_value = jnp.dot(normalized_input, value_weight, preferred_element_type=jnp.float32)
    query_matrix = apply_rotary(rms_scale(raw_query, q_gain), positions).astype(jnp.bfloat16)
    keys = apply_rotary(rms_scale(unrotated_key, k_gain), positions).astype(jnp.bfloat16)
    value_matrix = projected_value.astype(jnp.bfloat16).reshape(overall_rows, KEY_VALUE_HEADS, HEAD_DIM)
    prompt_q = query_matrix[:PROMPT_TOKENS]
    prompt_k = keys[:PROMPT_TOKENS]
    prompt_v = value_matrix[:PROMPT_TOKENS]
    token_index = jnp.arange(PROMPT_TOKENS, dtype=jnp.int32)
    causal = token_index[:, None] >= token_index[None, :]

    def one_head(head_index):
        query_head = lax.dynamic_index_in_dim(prompt_q, head_index, 1, keepdims=False)
        key_head = lax.dynamic_index_in_dim(prompt_k, head_index // query_group_width, 1, keepdims=False)
        value_head = lax.dynamic_index_in_dim(prompt_v, head_index // query_group_width, 1, keepdims=False)
        scores = jnp.dot(query_head, key_head.T, preferred_element_type=jnp.float32) * scaling
        scores = jnp.where(causal, scores, -1e+30)
        highest = lax.optimization_barrier(jnp.max(scores, axis=-1, keepdims=True))
        weights = jnp.where(causal, jnp.exp(scores - highest), 0.0)
        summed = jnp.dot(weights.astype(jnp.bfloat16), value_head, preferred_element_type=jnp.float32)
        return (summed / lax.optimization_barrier(jnp.sum(weights, axis=-1, keepdims=True))).astype(jnp.bfloat16)
    prompt_heads = lax.map(one_head, jnp.arange(QUERY_HEADS, dtype=jnp.int32))
    prompt_context = prompt_heads.transpose(1, 0, 2).reshape(PROMPT_TOKENS, QUERY_HEADS * HEAD_DIM)
    decode_query = query_matrix[PROMPT_TOKENS:].reshape(decode_rows, KEY_VALUE_HEADS, query_group_width, HEAD_DIM).astype(jnp.float32)
    step_k = keys[PROMPT_TOKENS:].astype(jnp.float32)
    step_v = value_matrix[PROMPT_TOKENS:].astype(jnp.float32)
    cache_scores = jnp.einsum('nkgd,pkd->nkgp', decode_query, prompt_k.astype(jnp.float32)) * scaling
    own_scores = jnp.einsum('nkgd,mkd->nkgm', decode_query, step_k) * scaling
    row_index = jnp.arange(decode_rows, dtype=jnp.int32)
    step_of = row_index // RESP
    resp_of = row_index % RESP
    allowed = (resp_of[:, None] == resp_of[None, :]) & (step_of[None, :] <= step_of[:, None])
    allowed = allowed[:, None, None, :]
    own_scores = jnp.where(allowed, own_scores, -1e+30)
    highest = jnp.maximum(lax.optimization_barrier(jnp.max(cache_scores, axis=-1)), lax.optimization_barrier(jnp.max(own_scores, axis=-1)))[..., None]
    cache_weights = jnp.exp(cache_scores - highest)
    own_weights = jnp.where(allowed, jnp.exp(own_scores - highest), 0.0)
    cache_rounded = lax.optimization_barrier(cache_weights.astype(jnp.bfloat16)).astype(jnp.float32)
    own_rounded = lax.optimization_barrier(own_weights.astype(jnp.bfloat16)).astype(jnp.float32)
    summed = jnp.einsum('nkgp,pkd->nkgd', cache_rounded, prompt_v.astype(jnp.float32))
    summed = summed + jnp.einsum('nkgm,mkd->nkgd', own_rounded, step_v)
    weight_sum = lax.optimization_barrier(jnp.sum(cache_weights, axis=-1)) + lax.optimization_barrier(jnp.sum(own_weights, axis=-1))
    step_context = (summed / weight_sum[..., None]).astype(jnp.bfloat16).reshape(STEPS, RESP, QUERY_HEADS * HEAD_DIM)
    return (prompt_context, step_context)
```

```python
import math

import jax
import jax.numpy as jnp
from jax import lax
from jax.sharding import PartitionSpec as P

QUERY_HEADS = 64
KEY_VALUE_HEADS = 8
HEAD_DIM = 128
EPS = 1e-06
THETA = 1000000.0
Z = 16
SEQ = 32
GRP = 16

Z_RINGS = [[2 * k + y for k in range(Z)] for y in range(2)]
Y_SWAP = [(i, i ^ 1) for i in range(SEQ)]
CORE_SWAP = [(i, i ^ 1) for i in range(GRP)]
STEP_HOME = [
    (g * SEQ + s, (s // 2) * SEQ + 2 * g + s % 2) for g in range(GRP) for s in range(SEQ)
]


def rms_scale(values_in, gain):
    return (
        values_in * lax.rsqrt(jnp.mean(values_in * values_in, axis=-1, keepdims=True) + EPS) * gain
    )


def rotary_tables(positions):
    half_size = HEAD_DIM // 2
    freqs = jnp.power(jnp.float32(THETA), -jnp.arange(half_size, dtype=jnp.float32) / half_size)
    angles = positions.astype(jnp.float32)[:, None] * freqs[None, :]
    return jnp.cos(angles), jnp.sin(angles)


def rotate(values_in, tables):
    cosine, sine = tables
    half_size = HEAD_DIM // 2
    first_half = values_in[..., :half_size]
    second_half = values_in[..., half_size:]
    return jnp.concatenate(
        [first_half * cosine - second_half * sine, second_half * cosine + first_half * sine],
        axis=-1,
    )


def pick(flag, when_true, when_false):
    return jnp.where(flag, when_true, when_false)


def ordered(flag, first, second, axis):
    return jnp.concatenate([pick(flag, first, second), pick(flag, second, first)], axis=axis)


def gather_z(block):
    return lax.all_gather(block, "seq", axis=0, tiled=True, axis_index_groups=Z_RINGS)


def depth_half(values_in, parity, depth):
    span = 2 * depth
    return jnp.concatenate(
        [
            pick(
                parity == 0,
                values_in[:, span * k : span * k + depth],
                values_in[:, span * k + depth : span * (k + 1)],
            )
            for k in range(Z)
        ],
        axis=1,
    )


def add_halves(partial, rows, steps):
    received = lax.ppermute(partial[: rows + steps], "seq", Y_SWAP)
    return partial[rows:] + jnp.roll(received, steps, axis=0)


def shards(
    prompt_states, step_states, norm_gain, w_query, key_weight, value_weight, q_gain, k_gain
):
    s = lax.axis_index("seq")
    g = lax.axis_index("grp")
    z = s // 2
    y = s % 2
    core = g % 2
    kv_head = g // 2
    rows = prompt_states.shape[0]
    width = prompt_states.shape[1]
    depth = w_query.shape[0]
    steps = step_states.shape[0]
    prompt_len = rows * SEQ
    scaling = 1.0 / math.sqrt(HEAD_DIM)

    q_weight = gather_z(w_query)

    key_cols = lax.dynamic_slice_in_dim(key_weight, kv_head * HEAD_DIM, HEAD_DIM, 1)
    value_cols = lax.dynamic_slice_in_dim(value_weight, kv_head * HEAD_DIM, HEAD_DIM, 1)
    kv_weight = gather_z(pick(core == 0, key_cols, value_cols))

    own_step = lax.dynamic_index_in_dim(step_states, z, 1, keepdims=False)
    x_own = rms_scale(prompt_states.astype(jnp.float32), norm_gain).astype(jnp.bfloat16)
    x_step = rms_scale(own_step.astype(jnp.float32), norm_gain).astype(jnp.bfloat16)
    x_partner = lax.ppermute(depth_half(x_own, 1 - y, depth), "seq", Y_SWAP)
    x_half = jnp.concatenate(
        [x_partner, depth_half(x_step, y, depth), depth_half(x_own, y, depth)], axis=0
    )

    step_pos = prompt_len + jnp.arange(steps, dtype=jnp.int32)
    row_iota = jnp.arange(rows, dtype=jnp.int32)
    own_pos = rows * s + row_iota
    raw_kv = add_halves(
        jnp.dot(x_half, kv_weight, preferred_element_type=jnp.float32), rows, steps
    )
    kv_tables = rotary_tables(jnp.concatenate([step_pos, own_pos]))
    keyed = rotate(rms_scale(raw_kv, k_gain), kv_tables)
    kv_type = pick(core == 0, keyed, raw_kv).astype(jnp.bfloat16)

    own_type = lax.all_to_all(
        jnp.broadcast_to(kv_type[steps:], (Z, rows, HEAD_DIM)),
        "seq",
        split_axis=0,
        concat_axis=0,
        axis_index_groups=Z_RINGS,
        tiled=True,
    ).reshape(Z * rows, HEAD_DIM)
    step_twin = lax.ppermute(kv_type[:steps], "grp", CORE_SWAP)

    own_type, step_twin = lax.optimization_barrier((own_type, step_twin))
    own_twin = lax.ppermute(own_type, "seq", Y_SWAP)
    other_type = lax.ppermute(own_type, "grp", CORE_SWAP)
    x_half, other_type = lax.optimization_barrier((x_half, other_type))
    partial = jnp.dot(x_half, q_weight, preferred_element_type=jnp.float32)
    own_twin, partial = lax.optimization_barrier((own_twin, partial))
    raw_query = add_halves(partial, rows, steps)
    step_heads = lax.dynamic_slice_in_dim(raw_query[:steps], y * 2 * HEAD_DIM, 2 * HEAD_DIM, 1)
    raw_query = jnp.concatenate(
        [
            raw_query[steps:].reshape(rows, 4, HEAD_DIM).transpose(1, 0, 2).reshape(-1, HEAD_DIM),
            step_heads.reshape(steps, 2, HEAD_DIM).transpose(1, 0, 2).reshape(-1, HEAD_DIM),
        ],
        axis=0,
    )
    query_pos = jnp.concatenate([own_pos, own_pos, own_pos, own_pos, step_pos, step_pos])
    query = rotate(rms_scale(raw_query, q_gain), rotary_tables(query_pos)).astype(jnp.bfloat16)

    other_twin = lax.ppermute(own_twin, "grp", CORE_SWAP)
    own_all = jnp.concatenate([own_type, own_twin, kv_type[:steps]], axis=0)
    other_all = jnp.concatenate([other_type, other_twin, step_twin], axis=0)
    cache_keys = pick(core == 0, own_all, other_all)
    cache_values = pick(core == 0, other_all, own_all)
    line = jnp.arange(rows * Z, dtype=jnp.int32)
    line_pos = line + rows * (line // rows)
    key_pos = jnp.concatenate([line_pos + rows * y, line_pos + rows * (1 - y), step_pos])

    scores = (
        jnp.einsum("rd,nd->rn", query, cache_keys, preferred_element_type=jnp.float32)
        * scaling
    )
    allowed = key_pos[None, :] <= query_pos[:, None]
    scores = jnp.where(allowed, scores, -1e30)
    highest = jnp.max(scores, axis=-1, keepdims=True)
    weights = jnp.where(allowed, jnp.exp(scores - highest), 0.0)
    weight_sum = jnp.sum(weights, axis=-1, keepdims=True)
    summed = jnp.dot(
        weights.astype(jnp.bfloat16), cache_values, preferred_element_type=jnp.float32
    )
    context = (summed / weight_sum).astype(jnp.bfloat16)
    prompt_context = context[: 4 * rows].reshape(4, rows, HEAD_DIM).transpose(1, 0, 2)
    step_context = context[4 * rows :].reshape(2, steps, HEAD_DIM).transpose(1, 0, 2)
    half_cols = 2 * HEAD_DIM
    step_out = lax.ppermute(step_context.reshape(steps, half_cols), ("grp", "seq"), STEP_HOME)
    prompt_context = prompt_context.reshape(rows, 4 * HEAD_DIM)
    return (prompt_context, step_out.reshape(steps, 1, half_cols))


def solution(mesh):
    placed = (P("seq", None), P(), P(), P("seq", "grp"), P("seq", None), P("seq", None), P(), P())
    return jax.shard_map(
        shards,
        mesh=mesh,
        in_specs=placed,
        out_specs=(P("seq", "grp"), P(None, "grp", "seq")),
        check_vma=False,
    )
```

```python
import math

import jax
import jax.numpy as jnp
from jax import lax
from jax.sharding import PartitionSpec as P

QUERY_HEADS = 64
KEY_VALUE_HEADS = 8
HEAD_DIM = 128
EPS = 1e-06
THETA = 1000000.0
Z = 16
SEQ = 32
GRP = 16

Z_RINGS = [[2 * k + y for k in range(Z)] for y in range(2)]
Y_SWAP = [(i, i ^ 1) for i in range(SEQ)]
CORE_SWAP = [(i, i ^ 1) for i in range(GRP)]
STEP_HOME = [
    (g * SEQ + s, (s // 2) * SEQ + 2 * g + s % 2) for g in range(GRP) for s in range(SEQ)
]


def rms_scale(values_in, gain):
    return (
        values_in * lax.rsqrt(jnp.mean(values_in * values_in, axis=-1, keepdims=True) + EPS) * gain
    )


def rotary_tables(positions):
    half_size = HEAD_DIM // 2
    freqs = jnp.power(jnp.float32(THETA), -jnp.arange(half_size, dtype=jnp.float32) / half_size)
    angles = positions.astype(jnp.float32)[:, None] * freqs[None, :]
    return jnp.cos(angles), jnp.sin(angles)


def rotate(values_in, tables):
    cosine, sine = tables
    half_size = HEAD_DIM // 2
    first_half = values_in[..., :half_size]
    second_half = values_in[..., half_size:]
    return jnp.concatenate(
        [first_half * cosine - second_half * sine, second_half * cosine + first_half * sine],
        axis=-1,
    )


def pick(flag, when_true, when_false):
    return jnp.where(flag, when_true, when_false)


def ordered(flag, first, second, axis):
    return jnp.concatenate([pick(flag, first, second), pick(flag, second, first)], axis=axis)


def gather_z(block):
    return lax.all_gather(block, "seq", axis=0, tiled=True, axis_index_groups=Z_RINGS)


def depth_half(values_in, parity, depth):
    span = 2 * depth
    return jnp.concatenate(
        [
            pick(
                parity == 0,
                values_in[:, span * k : span * k + depth],
                values_in[:, span * k + depth : span * (k + 1)],
            )
            for k in range(Z)
        ],
        axis=1,
    )


def add_halves(partial, rows, steps):
    received = lax.ppermute(partial[: rows + steps], "seq", Y_SWAP)
    return partial[rows:] + jnp.roll(received, steps, axis=0)


def shards(
    prompt_states, step_states, norm_gain, w_query, key_weight, value_weight, q_gain, k_gain
):
    s = lax.axis_index("seq")
    g = lax.axis_index("grp")
    z = s // 2
    y = s % 2
    core = g % 2
    kv_head = g // 2
    rows = prompt_states.shape[0]
    width = prompt_states.shape[1]
    depth = w_query.shape[0]
    steps = step_states.shape[0]
    prompt_len = rows * SEQ
    scaling = 1.0 / math.sqrt(HEAD_DIM)

    q_weight = gather_z(w_query)

    key_cols = lax.dynamic_slice_in_dim(key_weight, kv_head * HEAD_DIM, HEAD_DIM, 1)
    value_cols = lax.dynamic_slice_in_dim(value_weight, kv_head * HEAD_DIM, HEAD_DIM, 1)
    kv_weight = gather_z(pick(core == 0, key_cols, value_cols))

    own_step = lax.dynamic_index_in_dim(step_states, z, 1, keepdims=False)
    x_own = rms_scale(prompt_states.astype(jnp.float32), norm_gain).astype(jnp.bfloat16)
    x_step = rms_scale(own_step.astype(jnp.float32), norm_gain).astype(jnp.bfloat16)
    x_partner = lax.ppermute(depth_half(x_own, 1 - y, depth), "seq", Y_SWAP)
    x_half = jnp.concatenate(
        [x_partner, depth_half(x_step, y, depth), depth_half(x_own, y, depth)], axis=0
    )

    step_pos = prompt_len + jnp.arange(steps, dtype=jnp.int32)
    row_iota = jnp.arange(rows, dtype=jnp.int32)
    own_pos = rows * s + row_iota
    raw_kv = add_halves(
        jnp.dot(x_half, kv_weight, preferred_element_type=jnp.float32), rows, steps
    )
    kv_tables = rotary_tables(jnp.concatenate([step_pos, own_pos]))
    keyed = rotate(rms_scale(raw_kv, k_gain), kv_tables)
    kv_type = pick(core == 0, keyed, raw_kv).astype(jnp.bfloat16)

    own_type = lax.all_to_all(
        jnp.broadcast_to(kv_type[steps:], (Z, rows, HEAD_DIM)),
        "seq",
        split_axis=0,
        concat_axis=0,
        axis_index_groups=Z_RINGS,
        tiled=True,
    ).reshape(Z * rows, HEAD_DIM)
    step_twin = lax.ppermute(kv_type[:steps], "grp", CORE_SWAP)

    own_type, step_twin = lax.optimization_barrier((own_type, step_twin))
    own_twin = lax.ppermute(own_type, "seq", Y_SWAP)
    other_type = lax.ppermute(own_type, "grp", CORE_SWAP)
    x_half, other_type = lax.optimization_barrier((x_half, other_type))
    partial = jnp.dot(x_half, q_weight, preferred_element_type=jnp.float32)
    raw_query = add_halves(partial, rows, steps)
    step_heads = lax.dynamic_slice_in_dim(raw_query[:steps], y * 2 * HEAD_DIM, 2 * HEAD_DIM, 1)
    raw_query = jnp.concatenate(
        [
            raw_query[steps:].reshape(rows, 4, HEAD_DIM).transpose(1, 0, 2).reshape(-1, HEAD_DIM),
            step_heads.reshape(steps, 2, HEAD_DIM).transpose(1, 0, 2).reshape(-1, HEAD_DIM),
        ],
        axis=0,
    )
    query_pos = jnp.concatenate([own_pos, own_pos, own_pos, own_pos, step_pos, step_pos])
    query = rotate(rms_scale(raw_query, q_gain), rotary_tables(query_pos)).astype(jnp.bfloat16)

    other_twin = lax.ppermute(own_twin, "grp", CORE_SWAP)
    own_all = jnp.concatenate([own_type, own_twin, kv_type[:steps]], axis=0)
    other_all = jnp.concatenate([other_type, other_twin, step_twin], axis=0)
    cache_keys = pick(core == 0, own_all, other_all)
    cache_values = pick(core == 0, other_all, own_all)
    line = jnp.arange(rows * Z, dtype=jnp.int32)
    line_pos = line + rows * (line // rows)
    key_pos = jnp.concatenate([line_pos + rows * y, line_pos + rows * (1 - y), step_pos])

    scores = (
        jnp.einsum("rd,nd->rn", query, cache_keys, preferred_element_type=jnp.float32)
        * scaling
    )
    allowed = key_pos[None, :] <= query_pos[:, None]
    scores = jnp.where(allowed, scores, -1e30)
    highest = jnp.max(scores, axis=-1, keepdims=True)
    weights = jnp.where(allowed, jnp.exp(scores - highest), 0.0)
    weight_sum = jnp.sum(weights, axis=-1, keepdims=True)
    summed = jnp.dot(
        weights.astype(jnp.bfloat16), cache_values, preferred_element_type=jnp.float32
    )
    context = (summed / weight_sum).astype(jnp.bfloat16)
    prompt_context = context[: 4 * rows].reshape(4, rows, HEAD_DIM).transpose(1, 0, 2)
    step_context = context[4 * rows :].reshape(2, steps, HEAD_DIM).transpose(1, 0, 2)
    half_cols = 2 * HEAD_DIM
    step_out = lax.ppermute(step_context.reshape(steps, half_cols), ("grp", "seq"), STEP_HOME)
    prompt_context = prompt_context.reshape(rows, 4 * HEAD_DIM)
    return (prompt_context, step_out.reshape(steps, 1, half_cols))


def solution(mesh):
    placed = (P("seq", None), P(), P(), P("seq", "grp"), P("seq", None), P("seq", None), P(), P())
    return jax.shard_map(
        shards,
        mesh=mesh,
        in_specs=placed,
        out_specs=(P("seq", "grp"), P(None, "grp", "seq")),
        check_vma=False,
    )
```

```python
import math

import jax
import jax.numpy as jnp
from jax import lax
from jax.sharding import PartitionSpec as P

QUERY_HEADS = 64
KEY_VALUE_HEADS = 8
HEAD_DIM = 128
EPS = 1e-06
THETA = 1000000.0
Z = 16
SEQ = 32
GRP = 16

Z_RINGS = [[2 * k + y for k in range(Z)] for y in range(2)]
Y_SWAP = [(i, i ^ 1) for i in range(SEQ)]
CORE_SWAP = [(i, i ^ 1) for i in range(GRP)]
STEP_HOME = [
    (g * SEQ + s, (s // 2) * SEQ + 2 * g + s % 2) for g in range(GRP) for s in range(SEQ)
]


def rms_scale(values_in, gain):
    return (
        values_in * lax.rsqrt(jnp.mean(values_in * values_in, axis=-1, keepdims=True) + EPS) * gain
    )


def rotary_tables(positions):
    half_size = HEAD_DIM // 2
    freqs = jnp.power(jnp.float32(THETA), -jnp.arange(half_size, dtype=jnp.float32) / half_size)
    angles = positions.astype(jnp.float32)[:, None] * freqs[None, :]
    return jnp.cos(angles), jnp.sin(angles)


def rotate(values_in, tables):
    cosine, sine = tables
    half_size = HEAD_DIM // 2
    first_half = values_in[..., :half_size]
    second_half = values_in[..., half_size:]
    return jnp.concatenate(
        [first_half * cosine - second_half * sine, second_half * cosine + first_half * sine],
        axis=-1,
    )


def pick(flag, when_true, when_false):
    return jnp.where(flag, when_true, when_false)


def ordered(flag, first, second, axis):
    return jnp.concatenate([pick(flag, first, second), pick(flag, second, first)], axis=axis)


def gather_z(block):
    return lax.all_gather(block, "seq", axis=0, tiled=True, axis_index_groups=Z_RINGS)


def depth_half(values_in, parity, depth):
    span = 2 * depth
    return jnp.concatenate(
        [
            pick(
                parity == 0,
                values_in[:, span * k : span * k + depth],
                values_in[:, span * k + depth : span * (k + 1)],
            )
            for k in range(Z)
        ],
        axis=1,
    )


def add_halves(partial, rows, steps):
    received = lax.ppermute(partial[: rows + steps], "seq", Y_SWAP)
    return partial[rows:] + jnp.roll(received, steps, axis=0)


def shards(
    prompt_states, step_states, norm_gain, w_query, key_weight, value_weight, q_gain, k_gain
):
    s = lax.axis_index("seq")
    g = lax.axis_index("grp")
    z = s // 2
    y = s % 2
    core = g % 2
    kv_head = g // 2
    rows = prompt_states.shape[0]
    width = prompt_states.shape[1]
    depth = w_query.shape[0]
    steps = step_states.shape[0]
    prompt_len = rows * SEQ
    scaling = 1.0 / math.sqrt(HEAD_DIM)

    q_weight = gather_z(w_query)

    key_cols = lax.dynamic_slice_in_dim(key_weight, kv_head * HEAD_DIM, HEAD_DIM, 1)
    value_cols = lax.dynamic_slice_in_dim(value_weight, kv_head * HEAD_DIM, HEAD_DIM, 1)
    kv_weight = gather_z(pick(core == 0, key_cols, value_cols))

    own_step = lax.dynamic_index_in_dim(step_states, z, 1, keepdims=False)
    x_own = rms_scale(prompt_states.astype(jnp.float32), norm_gain).astype(jnp.bfloat16)
    x_step = rms_scale(own_step.astype(jnp.float32), norm_gain).astype(jnp.bfloat16)
    x_partner = lax.ppermute(depth_half(x_own, 1 - y, depth), "seq", Y_SWAP)
    x_half = jnp.concatenate(
        [x_partner, depth_half(x_step, y, depth), depth_half(x_own, y, depth)], axis=0
    )

    step_pos = prompt_len + jnp.arange(steps, dtype=jnp.int32)
    row_iota = jnp.arange(rows, dtype=jnp.int32)
    own_pos = rows * s + row_iota
    raw_kv = add_halves(
        jnp.dot(x_half, kv_weight, preferred_element_type=jnp.float32), rows, steps
    )
    kv_tables = rotary_tables(jnp.concatenate([step_pos, own_pos]))
    keyed = rotate(rms_scale(raw_kv, k_gain), kv_tables)
    kv_type = pick(core == 0, keyed, raw_kv).astype(jnp.bfloat16)

    own_type = lax.all_to_all(
        jnp.broadcast_to(kv_type[steps:], (Z, rows, HEAD_DIM)),
        "seq",
        split_axis=0,
        concat_axis=0,
        axis_index_groups=Z_RINGS,
        tiled=True,
    ).reshape(Z * rows, HEAD_DIM)
    step_twin = lax.ppermute(kv_type[:steps], "grp", CORE_SWAP)

    own_type, step_twin = lax.optimization_barrier((own_type, step_twin))
    own_twin = lax.ppermute(own_type, "seq", Y_SWAP)
    other_type = lax.ppermute(own_type, "grp", CORE_SWAP)
    x_half, other_type = lax.optimization_barrier((x_half, other_type))
    partial = jnp.dot(x_half, q_weight, preferred_element_type=jnp.float32)
    own_twin, raw_query = lax.optimization_barrier((own_twin, add_halves(partial, rows, steps)))
    step_heads = lax.dynamic_slice_in_dim(raw_query[:steps], y * 2 * HEAD_DIM, 2 * HEAD_DIM, 1)
    raw_query = jnp.concatenate(
        [
            raw_query[steps:].reshape(rows, 4, HEAD_DIM).transpose(1, 0, 2).reshape(-1, HEAD_DIM),
            step_heads.reshape(steps, 2, HEAD_DIM).transpose(1, 0, 2).reshape(-1, HEAD_DIM),
        ],
        axis=0,
    )
    query_pos = jnp.concatenate([own_pos, own_pos, own_pos, own_pos, step_pos, step_pos])
    query = rotate(rms_scale(raw_query, q_gain), rotary_tables(query_pos)).astype(jnp.bfloat16)

    other_twin = lax.ppermute(own_twin, "grp", CORE_SWAP)
    own_all = jnp.concatenate([own_type, own_twin, kv_type[:steps]], axis=0)
    other_all = jnp.concatenate([other_type, other_twin, step_twin], axis=0)
    cache_keys = pick(core == 0, own_all, other_all)
    cache_values = pick(core == 0, other_all, own_all)
    line = jnp.arange(rows * Z, dtype=jnp.int32)
    line_pos = line + rows * (line // rows)
    key_pos = jnp.concatenate([line_pos + rows * y, line_pos + rows * (1 - y), step_pos])

    scores = (
        jnp.einsum("rd,nd->rn", query, cache_keys, preferred_element_type=jnp.float32)
        * scaling
    )
    allowed = key_pos[None, :] <= query_pos[:, None]
    scores = jnp.where(allowed, scores, -1e30)
    highest = jnp.max(scores, axis=-1, keepdims=True)
    weights = jnp.where(allowed, jnp.exp(scores - highest), 0.0)
    weight_sum = jnp.sum(weights, axis=-1, keepdims=True)
    summed = jnp.dot(
        weights.astype(jnp.bfloat16), cache_values, preferred_element_type=jnp.float32
    )
    context = (summed / weight_sum).astype(jnp.bfloat16)
    prompt_context = context[: 4 * rows].reshape(4, rows, HEAD_DIM).transpose(1, 0, 2)
    step_context = context[4 * rows :].reshape(2, steps, HEAD_DIM).transpose(1, 0, 2)
    half_cols = 2 * HEAD_DIM
    step_out = lax.ppermute(step_context.reshape(steps, half_cols), ("grp", "seq"), STEP_HOME)
    prompt_context = prompt_context.reshape(rows, 4 * HEAD_DIM)
    return (prompt_context, step_out.reshape(steps, 1, half_cols))


def solution(mesh):
    placed = (P("seq", None), P(), P(), P("seq", "grp"), P("seq", None), P("seq", None), P(), P())
    return jax.shard_map(
        shards,
        mesh=mesh,
        in_specs=placed,
        out_specs=(P("seq", "grp"), P(None, "grp", "seq")),
        check_vma=False,
    )
```

```python
import math

import jax
import jax.numpy as jnp
from jax import lax
from jax.sharding import PartitionSpec as P

QUERY_HEADS = 64
KEY_VALUE_HEADS = 8
HEAD_DIM = 128
EPS = 1e-06
THETA = 1000000.0
Z = 16
SEQ = 32
GRP = 16

Z_RINGS = [[2 * k + y for k in range(Z)] for y in range(2)]
Y_SWAP = [(i, i ^ 1) for i in range(SEQ)]
CORE_SWAP = [(i, i ^ 1) for i in range(GRP)]
STEP_HOME = [
    (g * SEQ + s, (s // 2) * SEQ + 2 * g + s % 2) for g in range(GRP) for s in range(SEQ)
]


def rms_scale(values_in, gain):
    return (
        values_in * lax.rsqrt(jnp.mean(values_in * values_in, axis=-1, keepdims=True) + EPS) * gain
    )


def rotary_tables(positions):
    half_size = HEAD_DIM // 2
    freqs = jnp.power(jnp.float32(THETA), -jnp.arange(half_size, dtype=jnp.float32) / half_size)
    angles = positions.astype(jnp.float32)[:, None] * freqs[None, :]
    return jnp.cos(angles), jnp.sin(angles)


def rotate(values_in, tables):
    cosine, sine = tables
    half_size = HEAD_DIM // 2
    first_half = values_in[..., :half_size]
    second_half = values_in[..., half_size:]
    return jnp.concatenate(
        [first_half * cosine - second_half * sine, second_half * cosine + first_half * sine],
        axis=-1,
    )


def pick(flag, when_true, when_false):
    return jnp.where(flag, when_true, when_false)


def ordered(flag, first, second, axis):
    return jnp.concatenate([pick(flag, first, second), pick(flag, second, first)], axis=axis)


def gather_z(block):
    return lax.all_gather(block, "seq", axis=0, tiled=True, axis_index_groups=Z_RINGS)


def depth_half(values_in, parity, depth):
    span = 2 * depth
    return jnp.concatenate(
        [
            pick(
                parity == 0,
                values_in[:, span * k : span * k + depth],
                values_in[:, span * k + depth : span * (k + 1)],
            )
            for k in range(Z)
        ],
        axis=1,
    )


def add_halves(partial, rows, steps):
    received = lax.ppermute(partial[: rows + steps], "seq", Y_SWAP)
    return partial[rows:] + jnp.roll(received, steps, axis=0)


def shards(
    prompt_states, step_states, norm_gain, w_query, key_weight, value_weight, q_gain, k_gain
):
    s = lax.axis_index("seq")
    g = lax.axis_index("grp")
    z = s // 2
    y = s % 2
    core = g % 2
    kv_head = g // 2
    rows = prompt_states.shape[0]
    width = prompt_states.shape[1]
    depth = w_query.shape[0]
    steps = step_states.shape[0]
    prompt_len = rows * SEQ
    scaling = 1.0 / math.sqrt(HEAD_DIM)

    q_weight = gather_z(w_query)

    key_cols = lax.dynamic_slice_in_dim(key_weight, kv_head * HEAD_DIM, HEAD_DIM, 1)
    value_cols = lax.dynamic_slice_in_dim(value_weight, kv_head * HEAD_DIM, HEAD_DIM, 1)
    kv_weight = gather_z(pick(core == 0, key_cols, value_cols))

    own_step = lax.dynamic_index_in_dim(step_states, z, 1, keepdims=False)
    x_own = rms_scale(prompt_states.astype(jnp.float32), norm_gain).astype(jnp.bfloat16)
    x_step = rms_scale(own_step.astype(jnp.float32), norm_gain).astype(jnp.bfloat16)
    x_partner = lax.ppermute(depth_half(x_own, 1 - y, depth), "seq", Y_SWAP)
    x_half = jnp.concatenate(
        [x_partner, depth_half(x_step, y, depth), depth_half(x_own, y, depth)], axis=0
    )

    step_pos = prompt_len + jnp.arange(steps, dtype=jnp.int32)
    row_iota = jnp.arange(rows, dtype=jnp.int32)
    own_pos = rows * s + row_iota
    raw_kv = add_halves(
        jnp.dot(x_half, kv_weight, preferred_element_type=jnp.float32), rows, steps
    )
    kv_tables = rotary_tables(jnp.concatenate([step_pos, own_pos]))
    keyed = rotate(rms_scale(raw_kv, k_gain), kv_tables)
    kv_type = pick(core == 0, keyed, raw_kv).astype(jnp.bfloat16)

    own_type = lax.all_to_all(
        jnp.broadcast_to(kv_type[steps:], (Z, rows, HEAD_DIM)),
        "seq",
        split_axis=0,
        concat_axis=0,
        axis_index_groups=Z_RINGS,
        tiled=True,
    ).reshape(Z * rows, HEAD_DIM)
    step_twin = lax.ppermute(kv_type[:steps], "grp", CORE_SWAP)

    own_type, step_twin = lax.optimization_barrier((own_type, step_twin))
    own_twin = lax.ppermute(own_type, "seq", Y_SWAP)
    other_type = lax.ppermute(own_type, "grp", CORE_SWAP)
    x_half, other_type = lax.optimization_barrier((x_half, other_type))
    partial = jnp.dot(x_half, q_weight, preferred_element_type=jnp.float32)
    own_twin, raw_query = lax.optimization_barrier((own_twin, add_halves(partial, rows, steps)))
    step_heads = lax.dynamic_slice_in_dim(raw_query[:steps], y * 2 * HEAD_DIM, 2 * HEAD_DIM, 1)
    raw_query = jnp.concatenate(
        [
            raw_query[steps:].reshape(rows, 4, HEAD_DIM).transpose(1, 0, 2).reshape(-1, HEAD_DIM),
            step_heads.reshape(steps, 2, HEAD_DIM).transpose(1, 0, 2).reshape(-1, HEAD_DIM),
        ],
        axis=0,
    )
    query_pos = jnp.concatenate([own_pos, own_pos, own_pos, own_pos, step_pos, step_pos])
    query = rotate(rms_scale(raw_query, q_gain), rotary_tables(query_pos)).astype(jnp.bfloat16)

    other_twin = lax.ppermute(own_twin, "grp", CORE_SWAP)
    own_all = jnp.concatenate([own_type, own_twin, kv_type[:steps]], axis=0)
    other_all = jnp.concatenate([other_type, other_twin, step_twin], axis=0)
    cache_keys = pick(core == 0, own_all, other_all)
    cache_values = pick(core == 0, other_all, own_all)
    line = jnp.arange(rows * Z, dtype=jnp.int32)
    line_pos = line + rows * (line // rows)
    key_pos = jnp.concatenate([line_pos + rows * y, line_pos + rows * (1 - y), step_pos])

    def attend(query, query_pos):
        scores = (
            jnp.einsum("rd,nd->rn", query, cache_keys, preferred_element_type=jnp.float32)
            * scaling
        )
        allowed = key_pos[None, :] <= query_pos[:, None]
        scores = jnp.where(allowed, scores, -1e30)
        highest = jnp.max(scores, axis=-1, keepdims=True)
        weights = jnp.where(allowed, jnp.exp(scores - highest), 0.0)
        weight_sum = jnp.sum(weights, axis=-1, keepdims=True)
        summed = jnp.dot(
            weights.astype(jnp.bfloat16), cache_values, preferred_element_type=jnp.float32
        )
        return (summed / weight_sum).astype(jnp.bfloat16)

    step_context = attend(query[4 * rows :], query_pos[4 * rows :])
    step_context, query = lax.optimization_barrier((step_context, query[: 4 * rows]))
    step_context = step_context.reshape(2, steps, HEAD_DIM).transpose(1, 0, 2)
    half_cols = 2 * HEAD_DIM
    step_out = lax.ppermute(step_context.reshape(steps, half_cols), ("grp", "seq"), STEP_HOME)
    prompt_context = attend(query, query_pos[: 4 * rows])
    prompt_context = prompt_context.reshape(4, rows, HEAD_DIM).transpose(1, 0, 2)
    prompt_context = prompt_context.reshape(rows, 4 * HEAD_DIM)
    return (prompt_context, step_out.reshape(steps, 1, half_cols))


def solution(mesh):
    placed = (P("seq", None), P(), P(), P("seq", "grp"), P("seq", None), P("seq", None), P(), P())
    return jax.shard_map(
        shards,
        mesh=mesh,
        in_specs=placed,
        out_specs=(P("seq", "grp"), P(None, "grp", "seq")),
        check_vma=False,
    )
```
